128 devices in a mesh: gx: 4 (over x), gy: 32 (over z, y, core).
Axes of the slice: x: 4, y: 4, z: 4, core: 2. Of those that a mesh axis runs over, the one named last changes fastest.
Arguments:
- right_sides: bfloat16 [2048, 128, 256], P(('gx', 'gy')), may hold values from -6 to 6
- near_source: int32 [2048, 8], P(('gx', 'gy')), may hold values from 0 to 2047, as said below
- near_count: int32 [2048], P(('gx', 'gy')), may hold values from 2 to 8
- near_blocks: bfloat16 [2048, 8, 256, 256], P(('gx', 'gy')), may hold values from -0.125 to 0.125
- column_basis: bfloat16 [2048, 64, 256], P(('gx', 'gy')), may hold values from -0.375 to 0.375
- row_basis: bfloat16 [2048, 64, 256], P(('gx', 'gy')), may hold values from -0.75 to 0.75
- leaf_upward: bfloat16 [2048, 64, 64], P(('gx', 'gy')), may hold values from -0.25 to 0.25
- couple_source: int32 [2048, 8], P(('gx', 'gy')), may hold values from 0 to 2047, as said below
- couple_count: int32 [2048], P(('gx', 'gy')), may hold values from 1 to 8
- couple_blocks: bfloat16 [2048, 8, 64, 64], P(('gx', 'gy')), may hold values from -0.25 to 0.25
- mid_upward: bfloat16 [256, 64, 64], P(('gx', 'gy')), may hold values from -0.25 to 0.25
- mid_source: int32 [256, 4], P(('gx', 'gy')), may hold values from 0 to 255
- mid_blocks: bfloat16 [256, 4, 64, 64], P(('gx', 'gy')), may hold values from -0.375 to 0.375
- top_source: int32 [32, 4], replicated, may hold values from 0 to 31
- top_blocks: bfloat16 [32, 4, 64, 64], replicated, may hold values from -0.375 to 0.375
- mid_downward: bfloat16 [256, 64, 64], P(('gx', 'gy')), may hold values from -0.75 to 0.75
- leaf_downward: bfloat16 [2048, 64, 64], P(('gx', 'gy')), may hold values from -0.75 to 0.75
Outputs:
- product: bfloat16 [2048, 128, 256], P(('gx', 'gy'))
The draws below stay inside these ranges and needn't reach their ends.
Inputs may be any that keep to these rules, and one draw needn't show every extreme that they name: `near_source`: every entry lies within 8 of its row's leaf in Morton order; slot 0 is the leaf itself; slot 1 of an even leaf l is max(l - 8, 0) and of an odd leaf min(l + 8, 2047). `couple_source`: every entry lies at distance 2 to 8 from its row's leaf in Morton order, or is the first or last leaf; slot 0 of an even leaf l is max(l - 8, 0) and of an odd leaf min(l + 8, 2047).
All inputs are finite; a program needn't handle non-finite values.
Results may differ from the reference program's by a relative error of at most 0.0065.
Values may be sent and summed in bfloat16 or wider, within the bound.
A program may use at most 128 MiB of HBM per device.

```python
import jax
import jax.numpy as jnp
from jax import lax

PTS = 256
RANK = 64
NRHS = 128
NEAR = 8
COUPLE = 8
MID_COUPLE = 4
TOP_COUPLE = 4
REACH = 8
LEAVES = 2048
MIDS = 256
TOPS = 32


def banded(key, slots, lowest):
    key_mag, key_sign, key_row = jax.random.split(key, 3)
    magnitude = jax.random.randint(key_mag, (LEAVES, slots), lowest, REACH + 1)
    direction = jax.random.randint(key_sign, (LEAVES, slots), 0, 2) * 2 - 1
    target = jnp.arange(LEAVES, dtype=jnp.int32)[:, None]
    source = jnp.clip(target + magnitude * direction, 0, LEAVES - 1)
    row = jax.random.randint(key_row, (), REACH, LEAVES - REACH)
    source = source.at[row, slots - 1].set(row + REACH)
    return source.astype(jnp.int32)


def fixed_partner():
    target = jnp.arange(LEAVES, dtype=jnp.int32)
    step = target % 2 * 2 - 1
    return jnp.clip(target + step * REACH, 0, LEAVES - 1).astype(jnp.int32)


def counted(key, slots, lowest):
    key_count, key_top, key_low = jax.random.split(key, 3)
    count = jax.random.randint(key_count, (LEAVES,), lowest, slots + 1)
    count = count.at[jax.random.randint(key_top, (), 0, LEAVES)].set(slots)
    count = count.at[jax.random.randint(key_low, (), 0, LEAVES)].set(lowest)
    return count.astype(jnp.int32)


def draw_near_source(key, part):
    key = jax.random.fold_in(key, 11)
    source = banded(key, NEAR, 0)
    source = source.at[:, 0].set(jnp.arange(LEAVES, dtype=jnp.int32))
    return source.at[:, 1].set(fixed_partner())


def draw_near_count(key, part):
    key = jax.random.fold_in(key, 12)
    return counted(key, NEAR, 2)


def draw_couple_source(key, part):
    key = jax.random.fold_in(key, 13)
    source = banded(key, COUPLE, 2)
    return source.at[:, 0].set(fixed_partner())


def draw_couple_count(key, part):
    key = jax.random.fold_in(key, 14)
    return counted(key, COUPLE, 1)


def touch_ends(array, rng, low, largest):
    dims = array.shape
    index_at = [jax.random.randint(jax.random.fold_in(rng, axis), (), 0, dims[axis]) for axis in range(len(dims))]
    array = array.at[tuple(index_at)].set(low)
    longest = dims.index(max(dims))
    index_at[longest] = (index_at[longest] + 1) % dims[longest]
    return array.at[tuple(index_at)].set(largest)


def steps_of(rng, shape, cuts, smallest, top_value):
    level, own = 1.0, jax.random.fold_in(rng, 6)
    for position, shards_of in cuts:
        draws = jnp.exp(jax.random.uniform(jax.random.fold_in(own, position), (shards_of,), jnp.float32, smallest / len(cuts), top_value / len(cuts)))
        level = level * jnp.repeat(draws, shape[position] // shards_of).reshape([-1 if axis == position else 1 for axis in range(len(shape))])
    return level


def scatter_about(stream_key, dims, scale, limit, cuts=(), held_as=jnp.bfloat16):
    values = jax.random.normal(stream_key, dims, jnp.float32) * scale
    if len(cuts) > 0:
        values = steps_of(stream_key, dims, cuts, -0.22, 0.18) * values
    return jnp.clip(values, min=-limit, max=limit).astype(held_as)


def setup_inputs(seed: int = 0) -> dict:
    keys = jax.random.split(jax.random.key(seed), 18)
    return {
        "right_sides": scatter_about(keys[0], (LEAVES, NRHS, PTS), 1.0, 6.0, ((0, 128),)),
        "near_source": draw_near_source(jax.random.fold_in(keys[17], 71), 0),
        "near_count": draw_near_count(jax.random.fold_in(keys[17], 71), 0),
        "near_blocks": scatter_about(keys[3], (LEAVES, NEAR, PTS, PTS), (NEAR * PTS) ** -0.5, 0.125, ((0, 128),)),
        "column_basis": scatter_about(keys[4], (LEAVES, RANK, PTS), PTS ** -0.5, 0.375, ((0, 128),)),
        "row_basis": scatter_about(keys[5], (LEAVES, RANK, PTS), RANK ** -0.5, 0.75, ((0, 128),)),
        "leaf_upward": scatter_about(keys[6], (LEAVES, RANK, RANK), (8 * RANK) ** -0.5, 0.25, ((0, 128),)),
        "couple_source": draw_couple_source(jax.random.fold_in(keys[17], 71), 0),
        "couple_count": draw_couple_count(jax.random.fold_in(keys[17], 71), 0),
        "couple_blocks": scatter_about(keys[9], (LEAVES, COUPLE, RANK, RANK), (COUPLE * RANK) ** -0.5, 0.25, ((0, 128),)),
        "mid_upward": scatter_about(keys[10], (MIDS, RANK, RANK), (8 * RANK) ** -0.5, 0.25, ((0, 128),)),
        "mid_source": touch_ends(jax.random.randint(keys[11], (MIDS, MID_COUPLE), 0, MIDS), jax.random.fold_in(keys[11], 1), 0, MIDS - 1).astype(jnp.int32),
        "mid_blocks": scatter_about(keys[12], (MIDS, MID_COUPLE, RANK, RANK), (MID_COUPLE * RANK) ** -0.5, 0.375, ((0, 128),)),
        "top_source": touch_ends(jax.random.randint(keys[13], (TOPS, TOP_COUPLE), 0, TOPS), jax.random.fold_in(keys[13], 1), 0, TOPS - 1).astype(jnp.int32),
        "top_blocks": scatter_about(keys[14], (TOPS, TOP_COUPLE, RANK, RANK), (TOP_COUPLE * RANK) ** -0.5, 0.375),
        "mid_downward": scatter_about(keys[15], (MIDS, RANK, RANK), RANK ** -0.5, 0.75, ((0, 128),)),
        "leaf_downward": scatter_about(keys[16], (LEAVES, RANK, RANK), RANK ** -0.5, 0.75, ((0, 128),)),
    }


HIGH = lax.Precision.HIGHEST


def near_field(right_sides, near_source, near_count, near_blocks):
    width = 64

    def one_block(index):
        start = index * width
        source = lax.dynamic_slice_in_dim(near_source, start, width, 0)
        count = lax.dynamic_slice_in_dim(near_count, start, width, 0)
        blocks = lax.dynamic_slice_in_dim(near_blocks, start, width, 0).astype(jnp.float32)
        slots = jnp.arange(NEAR, dtype=jnp.int32)
        weight = (slots[None, :] < count[:, None]).astype(jnp.float32)
        picked = right_sides[source].astype(jnp.float32) * weight[:, :, None, None]
        return jnp.einsum('lnrq,lnpq->lrp', picked, blocks, precision=HIGH)

    result = lax.map(one_block, jnp.arange(LEAVES // width, dtype=jnp.int32))
    return result.reshape(LEAVES, NRHS, PTS)


def to_bf16(value):
    return lax.optimization_barrier(value.astype(jnp.bfloat16)).astype(jnp.float32)


def reference(right_sides, near_source, near_count, near_blocks, column_basis, row_basis, leaf_upward, couple_source, couple_count, couple_blocks, mid_upward, mid_source, mid_blocks, top_source, top_blocks, mid_downward, leaf_downward):
    near = near_field(right_sides, near_source, near_count, near_blocks)
    skeleton = to_bf16(jnp.einsum('lkp,lrp->lrk', column_basis.astype(jnp.float32), right_sides.astype(jnp.float32), precision=HIGH))
    slots = jnp.arange(COUPLE, dtype=jnp.int32)
    weight = (slots[None, :] < couple_count[:, None]).astype(jnp.float32)
    leaf_far = jnp.einsum('lcij,lcrj->lri', couple_blocks.astype(jnp.float32), skeleton[couple_source] * weight[:, :, None, None], precision=HIGH)
    raised = jnp.einsum('lij,lrj->lri', leaf_upward.astype(jnp.float32), skeleton, precision=HIGH)
    mid_skeleton = to_bf16(raised.reshape(MIDS, 8, NRHS, RANK).sum(axis=1))
    lifted = to_bf16(jnp.einsum('mij,mrj->mri', mid_upward.astype(jnp.float32), mid_skeleton, precision=HIGH))
    top_skeleton = lifted.reshape(TOPS, 8, NRHS, RANK).sum(axis=1)
    mid_far = jnp.einsum('mcij,mcrj->mri', mid_blocks.astype(jnp.float32), mid_skeleton[mid_source], precision=HIGH)
    top_far = jnp.einsum('ncij,ncrj->nri', top_blocks.astype(jnp.float32), top_skeleton[top_source], precision=HIGH)
    mid_local = mid_far + jnp.einsum('mij,mrj->mri', mid_downward.astype(jnp.float32), jnp.repeat(top_far, 8, axis=0), precision=HIGH)
    leaf_local = leaf_far + jnp.einsum('lij,lrj->lri', leaf_downward.astype(jnp.float32), jnp.repeat(mid_local, 8, axis=0), precision=HIGH)
    rounded = to_bf16(leaf_local)
    far = jnp.einsum('lkp,lrk->lrp', row_basis.astype(jnp.float32), rounded, precision=HIGH)
    return (near + far).astype(jnp.bfloat16)
```

```python
import functools

import jax
import jax.numpy as jnp
from jax import lax
from jax.experimental import pallas as pl
from jax.experimental.pallas import tpu as pltpu
from jax.sharding import PartitionSpec as P

MESH = pl.DeviceIdType.MESH
F32 = jnp.float32
BF16 = jnp.bfloat16
LINE = 4
PER = 10


def dot(a, b):
    return lax.dot_general(a, b, (((1,), (0,)), ((), ())), preferred_element_type=F32)


def dot_nt(a, b):
    return lax.dot_general(a, b, (((1,), (1,)), ((), ())), preferred_element_type=F32)


def dot_tn(a, b):
    return lax.dot_general(a, b, (((0,), (0,)), ((), ())), preferred_element_type=F32)


def kernel(
    rs_hbm, ns_hbm, nc_hbm, nb_hbm, cb_hbm, rb_hbm, lu_hbm, cs_hbm, cc_hbm, cp_hbm,
    mu_hbm, ms_hbm, mb_hbm, ts_hbm, tb_hbm, md_hbm, ld_hbm,
    out_hbm,
    rsw, nb, cb, rb, lu, cp, mu, mb, tb, md, ld,
    ns, nc, cs, cc, ts, mss, msv,
    skw, ust, cst, tst, qown, qin, qfull, mown, g1, g2, psend, precv,
    leaf_far, acc, outv,
    load_sem, nb_sem, out_sem,
    halo_send, halo_recv, skel_send, skel_recv, q_send, q_recv, i_send, i_recv,
    y_send, y_recv, g_send, g_recv, p_send, p_recv,
):
    x = lax.axis_index("gx")
    gy = lax.axis_index("gy")
    z = gy // 8
    y = (gy // 2) % 4
    c = gy % 2
    first = c == 0
    me = x * 32 + gy
    v = jnp.where(first, x, z)
    w = jnp.where(first, z, x)

    def on_line(place, core):
        return (jnp.where(first, place, x), jnp.where(first, z, place) * 8 + y * 2 + core)

    def on_gather(place):
        return (jnp.where(first, x, place), jnp.where(first, place, z) * 8 + y * 2 + c)

    def ring(step):
        d = lax.rem(me + step + 128, 128)
        return (d // 32, lax.rem(d, 32))

    sibling = (x, z * 8 + y * 2 + 1 - c)
    y_dev = lambda k: (x, z * 8 + lax.rem(y + k, 4) * 2 + c)
    x_dev = lambda k, core: (lax.rem(x + k, 4), z * 8 + y * 2 + core)
    z_dev = lambda k, core: (x, lax.rem(z + k, 4) * 8 + y * 2 + core)

    loads = {}

    def load(name, src, dst):
        loads[name] = pltpu.make_async_copy(src, dst, load_sem.at[len(loads)])
        loads[name].start()

    load("mb", mb_hbm, mb)
    load("md", md_hbm, md)
    load("rs", rs_hbm, rsw.at[pl.ds(8, 16)])
    load("cb", cb_hbm, cb)
    load("lu", lu_hbm, lu)
    load("mu", mu_hbm, mu)
    load("ns", ns_hbm, ns)
    load("nc", nc_hbm, nc)
    load("cs", cs_hbm, cs)
    load("cc", cc_hbm, cc)
    load("ts", ts_hbm, ts)
    load("ms", ms_hbm, msv.at[2 * v + c])
    for place in range(LINE):
        top = jnp.where(first, place * 8 + z * 2, x * 8 + place * 2) + y // 2
        load(f"tb{place}", tb_hbm.at[top], tb.at[place])
    load("cp", cp_hbm, cp)
    load("rb", rb_hbm, rb)
    load("ld", ld_hbm, ld)

    barrier = pltpu.get_barrier_semaphore()
    peers = [ring(1), ring(-1), sibling]
    for k in range(1, LINE):
        peers += [y_dev(k), x_dev(k, 0), x_dev(k, 1), z_dev(k, 0), z_dev(k, 1)]
    for peer in peers:
        pl.semaphore_signal(barrier, inc=1, device_id=peer, device_id_type=MESH)

    loads["mb"].wait()
    loads["md"].wait()
    for m in range(2):
        qown[:, 256 * m : 256 * m + 256] = jnp.concatenate([mb[m, k] for k in range(4)], axis=1)
    qown[:, 512:] = jnp.concatenate([md[0], md[1]], axis=1)
    loads["rs"].wait()
    pl.semaphore_wait(barrier, len(peers))

    def send(src, dst, send_sem, recv_sem, device):
        copy = pltpu.make_async_remote_copy(
            src_ref=src, dst_ref=dst, send_sem=send_sem, recv_sem=recv_sem,
            device_id=device, device_id_type=MESH,
        )
        copy.start()
        return copy

    sent = []
    halo = [
        send(rsw.at[pl.ds(8, 8)], rsw.at[pl.ds(24, 8)], halo_send.at[0], halo_recv.at[0], ring(-1)),
        send(rsw.at[pl.ds(16, 8)], rsw.at[pl.ds(0, 8)], halo_send.at[1], halo_recv.at[1], ring(1)),
    ]
    sent += halo
    slot0, slot1 = x * 2 + c, z * 2 + c
    for k in range(1, LINE):
        for core, device, slot in ((0, x_dev(k, 0), slot0), (1, z_dev(k, 1), slot1)):
            at = 2 * (k - 1) + core
            sem = 2 * (k - 1) + c
            sent.append(send(qown, qin.at[slot], q_send.at[at], q_recv.at[sem], device))
            sent.append(send(ms_hbm, msv.at[slot], i_send.at[at], i_recv.at[sem], device))
    slot = jnp.where(first, slot1, slot0)
    sent.append(send(qown, qin.at[slot], q_send.at[6], q_recv.at[6], sibling))
    sent.append(send(ms_hbm, msv.at[slot], i_send.at[6], i_recv.at[6], sibling))
    mine = 2 * v + c
    qin[mine] = qown[...]

    loads["cb"].wait()
    for t in range(16):
        pltpu.make_async_copy(nb_hbm.at[t], nb.at[t], nb_sem.at[t]).start()

    for l in range(16):
        skw[8 + l] = dot_nt(cb[l], rsw[8 + l]).astype(BF16)
    skel = [
        send(skw.at[pl.ds(8, 8)], skw.at[pl.ds(24, 8)], skel_send.at[0], skel_recv.at[0], ring(-1)),
        send(skw.at[pl.ds(16, 8)], skw.at[pl.ds(0, 8)], skel_send.at[1], skel_recv.at[1], ring(1)),
    ]
    sent += skel
    loads["lu"].wait()
    loads["mu"].wait()
    lift = None
    for m in range(2):
        upward = jnp.concatenate([lu[8 * m + l] for l in range(8)], axis=1)
        raised = dot(upward, skw[8 + 8 * m : 16 + 8 * m].reshape(512, 128)).astype(BF16)
        mown[m] = raised
        lifted = dot(mu[m], raised).astype(BF16).astype(F32)
        lift = lifted if lift is None else lift + lifted
    mown[2] = lift.astype(BF16)
    g1[y] = mown[...]
    gather1 = [send(mown, g1.at[y], y_send.at[k - 1], y_recv.at[k - 1], y_dev(k)) for k in range(1, LINE)]
    sent += gather1

    for place in range(LINE):
        loads[f"tb{place}"].wait()
        tst[place] = jnp.concatenate([tb[place, k] for k in range(4)], axis=1)
    loads["cp"].wait()
    for t in range(16):
        cst[t] = jnp.concatenate([cp[t, k] for k in range(8)], axis=1)

    for copy in gather1:
        copy.wait_recv()
    for p in range(4):
        for m in range(2):
            g2[w * PER + 2 * p + m] = g1[p, m]
    for h in range(2):
        g2[w * PER + 8 + h] = (g1[2 * h, 2].astype(F32) + g1[2 * h + 1, 2].astype(F32)).astype(BF16)
    part = g2.at[pl.ds(w * PER, PER)]
    gather2 = [
        send(part, part, g_send.at[k - 1], g_recv.at[k - 1], on_gather(lax.rem(w + k, LINE)))
        for k in range(1, LINE)
    ]
    sent += gather2

    for at in range(7):
        pltpu.make_async_remote_copy(
            src_ref=qown, dst_ref=qin.at[0], send_sem=q_send.at[at], recv_sem=q_recv.at[at],
            device_id=sibling, device_id_type=MESH,
        ).wait_recv()
        pltpu.make_async_remote_copy(
            src_ref=ms_hbm, dst_ref=msv.at[0], send_sem=i_send.at[at], recv_sem=i_recv.at[at],
            device_id=sibling, device_id_type=MESH,
        ).wait_recv()
    loads["ms"].wait()
    loads["ts"].wait()
    tables = pltpu.make_async_copy(msv, mss, out_sem.at[0])
    tables.start()
    lane = lax.broadcasted_iota(jnp.int32, (64, 128), 1)
    for s in range(8):
        down = qin[s, :, 512:]
        zero = jnp.zeros_like(down)
        both = jnp.concatenate([jnp.where(lane < 64, down, zero), jnp.where(lane < 64, zero, down)], axis=0)
        folded = dot(both, jnp.concatenate([tst[s // 2], tst[s // 2]], axis=0)).astype(BF16)
        for m in range(2):
            qfull[s, m, :, :256] = qin[s, :, 256 * m : 256 * m + 256]
            qfull[s, m, :, 256:] = folded[64 * m : 64 * m + 64]
    tables.wait()

    for copy in skel:
        copy.wait_recv()
    loads["cs"].wait()
    loads["cc"].wait()
    base = me * 16 - 8
    for t in range(16):
        rows = []
        for k in range(8):
            row = skw[jnp.clip(cs[k, t] - base, 0, 31)]
            rows.append(jnp.where(k < cc[t], row, jnp.zeros_like(row)))
        leaf_far[t] = dot(cst[t], jnp.concatenate(rows, axis=0))

    for copy in gather2:
        copy.wait_recv()

    def mid_row(m):
        dev = m // 2
        mx, mz, my, mc = dev // 32, (dev // 8) % 4, (dev // 2) % 4, dev % 2
        held = (mc == c) & (jnp.where(first, mx, mz) == v)
        row = g2[jnp.where(first, mz, mx) * PER + my * 2 + m % 2]
        return jnp.where(held, row, jnp.zeros_like(row))

    def top_row(n):
        nx, nz = n // 8, (n // 2) % 4
        row = g2[jnp.where(first, nz, nx) * PER + 8 + n % 2]
        return jnp.where(jnp.where(first, nx, nz) == v, row, jnp.zeros_like(row))

    for place in range(LINE):
        top = jnp.where(first, place * 8 + z * 2, x * 8 + place * 2) + y // 2
        tops = [top_row(ts[k, top]) for k in range(4)]
        for core in range(2):
            s = 2 * place + core
            for m in range(2):
                rows = [mid_row(mss[s, m, k]) for k in range(4)]
                psend[s, m] = dot(qfull[s, m], jnp.concatenate(rows + tops, axis=0)).astype(BF16)
    for k in range(1, LINE):
        place = lax.rem(v + k, LINE)
        for core in range(2):
            at = 2 * (k - 1) + core
            sent.append(
                send(psend.at[2 * place + core], precv.at[4 * c + v], p_send.at[at], p_recv.at[3 * c + k - 1],
                     on_line(place, core))
            )
    sent.append(send(psend.at[2 * v + 1 - c], precv.at[4 * c + v], p_send.at[6], p_recv.at[6], sibling))
    precv[4 * c + v] = psend[mine]

    for copy in halo:
        copy.wait_recv()
    loads["ns"].wait()
    loads["nc"].wait()

    def near(t, carry):
        pltpu.make_async_copy(nb_hbm.at[t], nb.at[t], nb_sem.at[t]).wait()
        total = jnp.zeros((128, 256), F32)
        for k in range(8):
            side = rsw[jnp.clip(ns[k, t] - base, 0, 31)]
            total += dot_nt(jnp.where(k < nc[t], side, jnp.zeros_like(side)), nb[t, k])
        acc[t] = total
        return carry

    lax.fori_loop(0, 16, near, 0)

    loads["ld"].wait()
    loads["rb"].wait()
    for at in range(7):
        pltpu.make_async_remote_copy(
            src_ref=psend.at[0], dst_ref=precv.at[0], send_sem=p_send.at[at], recv_sem=p_recv.at[at],
            device_id=sibling, device_id_type=MESH,
        ).wait_recv()
    copies = []
    for m in range(2):
        total = precv[0, m].astype(F32)
        for s in range(1, 8):
            total += precv[s, m].astype(F32)
        lowered = dot(ld[8 * m : 8 * m + 8].reshape(512, 64), total.astype(BF16))
        for l in range(8):
            t = 8 * m + l
            local = (leaf_far[t] + lowered[64 * l : 64 * l + 64]).astype(BF16)
            outv[t] = (acc[t] + dot_tn(local, rb[t])).astype(BF16)
        copy = pltpu.make_async_copy(
            outv.at[pl.ds(8 * m, 8)], out_hbm.at[pl.ds(8 * m, 8)], out_sem.at[1 + m]
        )
        copy.start()
        copies.append(copy)
    for copy in sent:
        copy.wait_send()
    for copy in copies:
        copy.wait()


def local(*args):
    args = list(args)
    for at in (1, 7, 13):
        args[at] = args[at].T
    vmem = pltpu.VMEM
    smem = pltpu.SMEM
    dma = pltpu.SemaphoreType.DMA
    scratch = [
        vmem((32, 128, 256), BF16),
        vmem((16, 8, 256, 256), BF16),
        vmem((16, 64, 256), BF16),
        vmem((16, 64, 256), BF16),
        vmem((16, 64, 64), BF16),
        vmem((16, 8, 64, 64), BF16),
        vmem((2, 64, 64), BF16),
        vmem((2, 4, 64, 64), BF16),
        vmem((4, 4, 64, 64), BF16),
        vmem((2, 64, 64), BF16),
        vmem((16, 64, 64), BF16),
        smem((8, 16), jnp.int32),
        smem((16,), jnp.int32),
        smem((8, 16), jnp.int32),
        smem((16,), jnp.int32),
        smem((4, 32), jnp.int32),
        smem((8, 2, 4), jnp.int32),
        vmem((8, 2, 4), jnp.int32),
        vmem((32, 64, 128), BF16),
        vmem((2, 64, 512), BF16),
        vmem((16, 64, 512), BF16),
        vmem((4, 64, 256), BF16),
        vmem((64, 640), BF16),
        vmem((8, 64, 640), BF16),
        vmem((8, 2, 64, 512), BF16),
        vmem((3, 64, 128), BF16),
        vmem((4, 3, 64, 128), BF16),
        vmem((4 * PER, 64, 128), BF16),
        vmem((8, 2, 64, 128), BF16),
        vmem((8, 2, 64, 128), BF16),
        vmem((16, 64, 128), F32),
        vmem((16, 128, 256), F32),
        vmem((16, 128, 256), BF16),
        dma((20,)), dma((16,)), dma((3,)),
        dma((2,)), dma((2,)), dma((2,)), dma((2,)),
        dma((7,)), dma((7,)), dma((7,)), dma((7,)),
        dma((3,)), dma((3,)), dma((3,)), dma((3,)),
        dma((7,)), dma((7,)),
    ]
    return pl.pallas_call(
        kernel,
        out_shape=jax.ShapeDtypeStruct((16, 128, 256), BF16),
        in_specs=[pl.BlockSpec(memory_space=pl.ANY)] * len(args),
        out_specs=pl.BlockSpec(memory_space=pl.ANY),
        scratch_shapes=scratch,
        compiler_params=pltpu.CompilerParams(
            collective_id=0, has_side_effects=True, vmem_limit_bytes=56 * 1024 * 1024
        ),
    )(*args)


def solution(mesh):
    both = ("gx", "gy")
    placed = [P(both)] * 17
    placed[13] = placed[14] = P()
    return jax.shard_map(
        local, mesh=mesh, in_specs=tuple(placed), out_specs=P(both), check_vma=False
    )
```

```python
import functools

import jax
import jax.numpy as jnp
from jax import lax
from jax.experimental import pallas as pl
from jax.experimental.pallas import tpu as pltpu
from jax.sharding import PartitionSpec as P

MESH = pl.DeviceIdType.MESH
F32 = jnp.float32
BF16 = jnp.bfloat16
LINE = 4
PER = 10


def dot(a, b):
    return lax.dot_general(a, b, (((1,), (0,)), ((), ())), preferred_element_type=F32)


def dot_nt(a, b):
    return lax.dot_general(a, b, (((1,), (1,)), ((), ())), preferred_element_type=F32)


def dot_tn(a, b):
    return lax.dot_general(a, b, (((0,), (0,)), ((), ())), preferred_element_type=F32)


def kernel(
    rs_hbm, ns_hbm, nc_hbm, nb_hbm, cb_hbm, rb_hbm, lu_hbm, cs_hbm, cc_hbm, cp_hbm,
    mu_hbm, ms_hbm, mb_hbm, ts_hbm, tb_hbm, md_hbm, ld_hbm,
    out,
    rlo, rhi, nb, cb, rb, lu, cp, mu, mb, tb, md, ld,
    ns, nc, cs, cc, ts, mss, mix, tix, msv,
    skw, ust, cst, tst, qown, qin, qfull, mown, g1, g2, psend, precv,
    leaf_far, acc,
    load_sem, nb_sem, out_sem,
    halo_send, halo_recv, skel_send, skel_recv, q_send, q_recv, i_send, i_recv,
    y_send, y_recv, g_send, g_recv, p_send, p_recv,
):
    x = lax.axis_index("gx")
    gy = lax.axis_index("gy")
    z = gy // 8
    y = (gy // 2) % 4
    c = gy % 2
    first = c == 0
    me = x * 32 + gy
    def along_x(core):
        return core == 0

    def pick(a, b):
        return jnp.where(along_x(c), a, b)

    v = pick(x, z)
    w = pick(z, x)

    def on_line(place, core):
        return (pick(place, x), pick(z, place) * 8 + y * 2 + core)

    def on_gather(place):
        return (pick(x, place), pick(place, z) * 8 + y * 2 + c)

    def ring(step):
        d = lax.rem(me + step + 128, 128)
        return (d // 32, lax.rem(d, 32))

    sibling = (x, z * 8 + y * 2 + 1 - c)
    y_dev = lambda k: (x, z * 8 + lax.rem(y + k, 4) * 2 + c)
    x_dev = lambda k, core: (lax.rem(x + k, 4), z * 8 + y * 2 + core)
    z_dev = lambda k, core: (x, lax.rem(z + k, 4) * 8 + y * 2 + core)

    def send(src, dst, send_sem, recv_sem, device):
        copy = pltpu.make_async_remote_copy(
            src_ref=src, dst_ref=dst, send_sem=send_sem, recv_sem=recv_sem,
            device_id=device, device_id_type=MESH,
        )
        copy.start()
        return copy

    def arrived(src, dst, send_sem, recv_sem):
        pltpu.make_async_remote_copy(
            src_ref=src, dst_ref=dst, send_sem=send_sem, recv_sem=recv_sem,
            device_id=sibling, device_id_type=MESH,
        ).wait_recv()

    loads = {}

    def load(name, src, dst):
        loads[name] = pltpu.make_async_copy(src, dst, load_sem.at[len(loads)])
        loads[name].start()

    load("rs", rs_hbm, rlo.at[pl.ds(8, 16)])
    load("cb", cb_hbm, cb)
    load("lu", lu_hbm, lu)
    load("mu", mu_hbm, mu)
    load("mb", mb_hbm, mb)
    load("md", md_hbm, md)

    barrier = pltpu.get_barrier_semaphore()
    peers = [sibling]
    for k in range(1, LINE):
        peers += [y_dev(k), x_dev(k, 0), x_dev(k, 1), z_dev(k, 0), z_dev(k, 1)]
    for peer in peers:
        pl.semaphore_signal(barrier, inc=1, device_id=peer, device_id_type=MESH)

    @pl.when(me > 0)
    def _():
        pl.semaphore_signal(barrier, inc=1, device_id=ring(-1), device_id_type=MESH)

    @pl.when(me < 127)
    def _():
        pl.semaphore_signal(barrier, inc=1, device_id=ring(1), device_id_type=MESH)

    expected = len(peers) + jnp.where(me > 0, 1, 0) + jnp.where(me < 127, 1, 0)

    def start_rest():
        load("rs2", rs_hbm, rhi.at[pl.ds(0, 16)])
        load("ns", ns_hbm, ns)
        load("nc", nc_hbm, nc)
        load("cs", cs_hbm, cs)
        load("cc", cc_hbm, cc)
        load("ts", ts_hbm, ts)
        load("ms", ms_hbm, msv.at[mine])
        load("cp", cp_hbm, cp)
        for place in range(LINE):
            load(f"tb{place}", tb_hbm.at[top_of(place)], tb.at[place])
        load("ld", ld_hbm, ld)
        load("rb", rb_hbm, rb)
        for t in range(16):
            pltpu.make_async_copy(nb_hbm.at[t], nb.at[t], nb_sem.at[t]).start()

    def top_of(place):
        return pick(place * 8 + z * 2, x * 8 + place * 2) + y // 2

    def skeletons():
        for l in range(16):
            skw[8 + l] = dot_nt(cb[l], rlo[8 + l]).astype(BF16)
        loads["mu"].wait()
        lift = None
        for m in range(2):
            raised = dot(ust[m], skw[8 + 8 * m : 16 + 8 * m].reshape(512, 128)).astype(BF16)
            mown[m] = raised
            lifted = dot(mu[m], raised).astype(BF16).astype(F32)
            lift = lifted if lift is None else lift + lifted
        mown[2] = lift.astype(BF16)

    def send_y():
        copies["y"] = [
            send(mown, g1.at[y], y_send.at[k - 1], y_recv.at[k - 1], y_dev(k)) for k in range(1, LINE)
        ]

    def send_skel():
        copies["skel"] = exchange(skw, skw, 24, skel_send, skel_recv)

    def send_halo():
        copies["halo"] = exchange(rlo, rhi, 16, halo_send, halo_recv)

    def exchange(window, above, at, send_sem, recv_sem):
        down = pltpu.make_async_remote_copy(
            src_ref=window.at[pl.ds(8, 8)], dst_ref=above.at[pl.ds(at, 8)],
            send_sem=send_sem.at[0], recv_sem=recv_sem.at[0], device_id=ring(-1), device_id_type=MESH,
        )
        up = pltpu.make_async_remote_copy(
            src_ref=window.at[pl.ds(16, 8)], dst_ref=window.at[pl.ds(0, 8)],
            send_sem=send_sem.at[1], recv_sem=recv_sem.at[1], device_id=ring(1), device_id_type=MESH,
        )
        pl.when(gy % 8 != 0)(down.start)
        pl.when(gy % 8 != 7)(up.start)
        return down, up

    def send_late(name):
        down, up = copies[name]
        pl.when(jnp.logical_and(gy % 8 == 0, me > 0))(down.start)
        pl.when(jnp.logical_and(gy % 8 == 7, me < 127))(up.start)

    def wait_window(name):
        down, up = copies[name]
        pl.when(me < 127)(down.wait_recv)
        pl.when(me > 0)(up.wait_recv)

    def stack_q():
        loads["mb"].wait()
        loads["md"].wait()
        for m in range(2):
            qown[:, 256 * m : 256 * m + 256] = jnp.concatenate([mb[m, k] for k in range(4)], axis=1)
        qown[:, 512:] = jnp.concatenate([md[0], md[1]], axis=1)

    def send_q():
        slot0, slot1 = x * 2 + c, z * 2 + c
        for k in range(1, LINE):
            for core in range(2):
                device = tuple(jnp.where(along_x(core), a, b) for a, b in zip(x_dev(k, core), z_dev(k, core)))
                slot = jnp.where(along_x(core), slot0, slot1)
                at = 2 * (k - 1) + core
                sem = 2 * (k - 1) + c
                sent.append(send(qown, qin.at[slot], q_send.at[at], q_recv.at[sem], device))
                sent.append(send(ms_hbm, msv.at[slot], i_send.at[at], i_recv.at[sem], device))
        slot = jnp.where(along_x(1 - c), slot0, slot1)
        sent.append(send(qown, qin.at[slot], q_send.at[6], q_recv.at[6], sibling))
        sent.append(send(ms_hbm, msv.at[slot], i_send.at[6], i_recv.at[6], sibling))
        qin[mine] = qown[...]

    def stack_t():
        for place in range(LINE):
            loads[f"tb{place}"].wait()
            tst[place] = jnp.concatenate([tb[place, k] for k in range(4)], axis=1)

    def send_g():
        g1[y] = mown[...]
        for copy in copies["y"]:
            copy.wait_recv()
        for p in range(4):
            for m in range(2):
                g2[w * PER + 2 * p + m] = g1[p, m]
        for h in range(2):
            g2[w * PER + 8 + h] = (g1[2 * h, 2].astype(F32) + g1[2 * h + 1, 2].astype(F32)).astype(BF16)
        half = PER // 2
        up, down = on_gather(lax.rem(w + 1, LINE)), on_gather(lax.rem(w + 3, LINE))
        low, high = g2.at[pl.ds(w * PER, half)], g2.at[pl.ds(w * PER + half, half)]
        copies["g"] = [
            send(part, part, g_send.at[at], g_recv.at[at], device)
            for at, (part, device) in enumerate(((low, up), (high, down), (high, up), (low, down)))
        ]

    def forward_g():
        half = PER // 2
        up, down = on_gather(lax.rem(w + 1, LINE)), on_gather(lax.rem(w + 3, LINE))
        for at, place, start, device in ((0, w + 3, 0, up), (1, w + 1, half, down)):
            copies["g"][at].wait_recv()
            part = g2.at[pl.ds(lax.rem(place, LINE) * PER + start, half)]
            copies["g"].append(send(part, part, g_send.at[4 + at], g_recv.at[4 + at], device))

    def stack_c():
        loads["cp"].wait()
        for t in range(16):
            cst[t] = jnp.concatenate([cp[t, k] for k in range(8)], axis=1)

    def couple():
        wait_window("skel")
        loads["cs"].wait()
        loads["cc"].wait()
        for t in range(16):
            rows = []
            for k in range(8):
                row = skw[jnp.clip(cs[k, t] - base, 0, 31)]
                rows.append(jnp.where(k < cc[t], row, jnp.zeros_like(row)))
            leaf_far[t] = dot(cst[t], jnp.concatenate(rows, axis=0))

    def fold():
        for at in range(7):
            arrived(qown, qin.at[0], q_send.at[at], q_recv.at[at])
            arrived(ms_hbm, msv.at[0], i_send.at[at], i_recv.at[at])
        loads["ms"].wait()
        loads["ts"].wait()
        tables = pltpu.make_async_copy(msv, mss, out_sem.at[0])
        tables.start()
        lane = lax.broadcasted_iota(jnp.int32, (64, 128), 1)
        for s in range(8):
            down = qin[s, :, 512:]
            zero = jnp.zeros_like(down)
            both = jnp.concatenate(
                [jnp.where(lane < 64, down, zero), jnp.where(lane < 64, zero, down)], axis=0
            )
            folded = dot(both, jnp.concatenate([tst[s // 2], tst[s // 2]], axis=0)).astype(BF16)
            for m in range(2):
                qfull[s, m, :, :256] = qin[s, :, 256 * m : 256 * m + 256]
                qfull[s, m, :, 256:] = folded[64 * m : 64 * m + 64]
        tables.wait()
        g2[LINE * PER] = jnp.zeros((64, 128), BF16)
        for i in range(4):
            for s in range(8):
                for m in range(2):
                    mix[s, m, i] = mid_at(mss[s, m, i])
            for place in range(LINE):
                tix[place, i] = top_at(ts[i, top_of(place)])

    def near(window, start, shift):
        def step(i, carry):
            t = start + i
            total = jnp.zeros((128, 256), F32)
            for k in range(8):
                side = window[jnp.clip(ns[k, t] - shift, 0, 23)]
                total += dot_nt(jnp.where(k < nc[t], side, jnp.zeros_like(side)), nb[t, k])
            acc[t] = total
            return carry

        lax.fori_loop(0, 8, step, 0)

    def near_low():
        pl.when(me > 0)(copies["halo"][1].wait_recv)
        near(rlo, 0, me * 16 - 8)

    def near_high():
        pl.when(me < 127)(copies["halo"][0].wait_recv)
        near(rhi, 8, me * 16)

    def near_fast():
        pl.when(first)(near_high)
        pl.when(c == 1)(near_low)

    def near_slow():
        pl.when(first)(near_low)
        pl.when(c == 1)(near_high)

    def wait_near():
        loads["rs2"].wait()
        loads["ns"].wait()
        loads["nc"].wait()
        for t in range(16):
            pltpu.make_async_copy(nb_hbm.at[t], nb.at[t], nb_sem.at[t]).wait()

    def mid_at(m):
        dev = m // 2
        mx, mz, my, mc = dev // 32, (dev // 8) % 4, (dev // 2) % 4, dev % 2
        held = (mc == c) & (pick(mx, mz) == v)
        return jnp.where(held, pick(mz, mx) * PER + my * 2 + m % 2, LINE * PER)

    def top_at(n):
        nx, nz = n // 8, (n // 2) % 4
        return jnp.where(pick(nx, nz) == v, pick(nz, nx) * PER + 8 + n % 2, LINE * PER)

    def serve():
        for copy in copies["g"][2:]:
            copy.wait_recv()
        for k in range(1, LINE + 1):
            place = lax.rem(v + k, LINE)
            tops = [g2[tix[place, i]] for i in range(4)]
            for core in range(2):
                s = 2 * place + core
                for m in range(2):
                    rows = [g2[mix[s, m, i]] for i in range(4)]
                    psend[s, m] = dot(qfull[s, m], jnp.concatenate(rows + tops, axis=0)).astype(BF16)
                if k < LINE:
                    at = 2 * (k - 1) + core
                    sent.append(
                        send(psend.at[s], precv.at[4 * c + v], p_send.at[at], p_recv.at[3 * c + k - 1],
                             on_line(place, core))
                    )
        sent.append(
            send(psend.at[2 * v + 1 - c], precv.at[4 * c + v], p_send.at[6], p_recv.at[6], sibling)
        )
        precv[4 * c + v] = psend[mine]

    def lower():
        loads["ld"].wait()
        loads["rb"].wait()
        for at in range(7):
            arrived(psend.at[0], precv.at[0], p_send.at[at], p_recv.at[at])
        for m in range(2):
            total = precv[0, m].astype(F32)
            for s in range(1, 8):
                total += precv[s, m].astype(F32)
            lowered = dot(ld[8 * m : 8 * m + 8].reshape(512, 64), total.astype(BF16))
            for l in range(8):
                t = 8 * m + l
                local = (leaf_far[t] + lowered[64 * l : 64 * l + 64]).astype(BF16)
                out[t] = (acc[t] + dot_tn(local, rb[t])).astype(BF16)

    def finish():
        for copy in sent + copies["y"] + copies["g"]:
            copy.wait_send()
        for name in ("skel", "halo"):
            down, up = copies[name]
            pl.when(me > 0)(down.wait_send)
            pl.when(me < 127)(up.wait_send)

    copies, sent = {}, []
    mine = 2 * v + c
    base = me * 16 - 8
    loads["lu"].wait()
    for m in range(2):
        ust[m] = jnp.concatenate([lu[8 * m + l] for l in range(8)], axis=1)
    loads["rs"].wait()
    loads["cb"].wait()
    start_rest()
    skeletons()
    pl.semaphore_wait(barrier, expected)
    send_y()
    send_halo()
    send_skel()
    send_late("skel")
    stack_q()
    send_q()
    stack_t()
    send_g()
    stack_c()
    forward_g()
    send_late("halo")
    fold()
    pl.when(z <= 2)(wait_near)
    pl.when(z <= 2)(near_fast)
    serve()
    pl.when(z > 2)(wait_near)
    pl.when(z > 2)(near_fast)
    near_slow()
    couple()
    lower()
    finish()


def local(*args):
    args = list(args)
    for at in (1, 7, 13):
        args[at] = args[at].T
    vmem = pltpu.VMEM
    smem = pltpu.SMEM
    dma = pltpu.SemaphoreType.DMA
    scratch = [
        vmem((24, 128, 256), BF16),
        vmem((24, 128, 256), BF16),
        vmem((16, 8, 256, 256), BF16),
        vmem((16, 64, 256), BF16),
        vmem((16, 64, 256), BF16),
        vmem((16, 64, 64), BF16),
        vmem((16, 8, 64, 64), BF16),
        vmem((2, 64, 64), BF16),
        vmem((2, 4, 64, 64), BF16),
        vmem((4, 4, 64, 64), BF16),
        vmem((2, 64, 64), BF16),
        vmem((16, 64, 64), BF16),
        smem((8, 16), jnp.int32),
        smem((16,), jnp.int32),
        smem((8, 16), jnp.int32),
        smem((16,), jnp.int32),
        smem((4, 32), jnp.int32),
        smem((8, 2, 4), jnp.int32),
        smem((8, 2, 4), jnp.int32),
        smem((4, 4), jnp.int32),
        vmem((8, 2, 4), jnp.int32),
        vmem((32, 64, 128), BF16),
        vmem((2, 64, 512), BF16),
        vmem((16, 64, 512), BF16),
        vmem((4, 64, 256), BF16),
        vmem((64, 640), BF16),
        vmem((8, 64, 640), BF16),
        vmem((8, 2, 64, 512), BF16),
        vmem((3, 64, 128), BF16),
        vmem((4, 3, 64, 128), BF16),
        vmem((4 * PER + 1, 64, 128), BF16),
        vmem((8, 2, 64, 128), BF16),
        vmem((8, 2, 64, 128), BF16),
        vmem((16, 64, 128), F32),
        vmem((16, 128, 256), F32),
        dma((20,)), dma((16,)), dma((1,)),
        dma((2,)), dma((2,)), dma((2,)), dma((2,)),
        dma((7,)), dma((7,)), dma((7,)), dma((7,)),
        dma((3,)), dma((3,)), dma((6,)), dma((6,)),
        dma((7,)), dma((7,)),
    ]
    return pl.pallas_call(
        kernel,
        out_shape=jax.ShapeDtypeStruct((16, 128, 256), BF16),
        in_specs=[pl.BlockSpec(memory_space=pl.ANY)] * len(args),
        out_specs=pl.BlockSpec(memory_space=pltpu.VMEM),
        scratch_shapes=scratch,
        compiler_params=pltpu.CompilerParams(
            collective_id=0, has_side_effects=True, vmem_limit_bytes=56 * 1024 * 1024
        ),
    )(*args)


def solution(mesh):
    both = ("gx", "gy")
    placed = [P(both)] * 17
    placed[13] = placed[14] = P()
    return jax.shard_map(
        local, mesh=mesh, in_specs=tuple(placed), out_specs=P(both), check_vma=False
    )
```

```python
import functools

import jax
import jax.numpy as jnp
from jax import lax
from jax.experimental import pallas as pl
from jax.experimental.pallas import tpu as pltpu
from jax.sharding import PartitionSpec as P

MESH = pl.DeviceIdType.MESH
F32 = jnp.float32
BF16 = jnp.bfloat16
LINE = 4
PER = 10


def dot(a, b):
    return lax.dot_general(a, b, (((1,), (0,)), ((), ())), preferred_element_type=F32)


def dot_nt(a, b):
    return lax.dot_general(a, b, (((1,), (1,)), ((), ())), preferred_element_type=F32)


def dot_tn(a, b):
    return lax.dot_general(a, b, (((0,), (0,)), ((), ())), preferred_element_type=F32)


def kernel(
    rs_hbm, ns_hbm, nc_hbm, nb_hbm, cb_hbm, rb_hbm, lu_hbm, cs_hbm, cc_hbm, cp_hbm,
    mu_hbm, ms_hbm, mb_hbm, ts_hbm, tb_hbm, md_hbm, ld_hbm,
    out,
    rlo, rhi, nb, cb, rb, lu, cp, mu, mb, tb, md, ld,
    ns, nc, cs, cc, ts, mss, mix, tix, msv,
    skw, ust, cst, tst, qown, qin, qfull, mown, g1, g2, psend, precv,
    leaf_far, acc,
    load_sem, nb_sem, out_sem,
    halo_send, halo_recv, skel_send, skel_recv, q_send, q_recv, i_send, i_recv,
    y_send, y_recv, g_send, g_recv, p_send, p_recv,
):
    x = lax.axis_index("gx")
    gy = lax.axis_index("gy")
    z = gy // 8
    y = (gy // 2) % 4
    c = gy % 2
    first = c == 0
    me = x * 32 + gy
    def along_x(core):
        return core == 0

    def pick(a, b):
        return jnp.where(along_x(c), a, b)

    v = pick(x, z)
    w = pick(z, x)

    def on_line(place, core):
        return (pick(place, x), pick(z, place) * 8 + y * 2 + core)

    def on_gather(place):
        return (pick(x, place), pick(place, z) * 8 + y * 2 + c)

    def ring(step):
        d = lax.rem(me + step + 128, 128)
        return (d // 32, lax.rem(d, 32))

    sibling = (x, z * 8 + y * 2 + 1 - c)
    y_dev = lambda k: (x, z * 8 + lax.rem(y + k, 4) * 2 + c)
    x_dev = lambda k, core: (lax.rem(x + k, 4), z * 8 + y * 2 + core)
    z_dev = lambda k, core: (x, lax.rem(z + k, 4) * 8 + y * 2 + core)

    def send(src, dst, send_sem, recv_sem, device):
        copy = pltpu.make_async_remote_copy(
            src_ref=src, dst_ref=dst, send_sem=send_sem, recv_sem=recv_sem,
            device_id=device, device_id_type=MESH,
        )
        copy.start()
        return copy

    def arrived(src, dst, send_sem, recv_sem):
        pltpu.make_async_remote_copy(
            src_ref=src, dst_ref=dst, send_sem=send_sem, recv_sem=recv_sem,
            device_id=sibling, device_id_type=MESH,
        ).wait_recv()

    loads = {}

    def load(name, src, dst):
        loads[name] = pltpu.make_async_copy(src, dst, load_sem.at[len(loads)])
        loads[name].start()

    load("rs", rs_hbm, rlo.at[pl.ds(8, 16)])
    load("cb", cb_hbm, cb)
    load("lu", lu_hbm, lu)
    load("mu", mu_hbm, mu)
    load("mb", mb_hbm, mb)
    load("md", md_hbm, md)

    barrier = pltpu.get_barrier_semaphore()
    peers = [sibling]
    for k in range(1, LINE):
        peers += [y_dev(k), x_dev(k, 0), x_dev(k, 1), z_dev(k, 0), z_dev(k, 1)]
    for peer in peers:
        pl.semaphore_signal(barrier, inc=1, device_id=peer, device_id_type=MESH)

    @pl.when(me > 0)
    def _():
        pl.semaphore_signal(barrier, inc=1, device_id=ring(-1), device_id_type=MESH)

    @pl.when(me < 127)
    def _():
        pl.semaphore_signal(barrier, inc=1, device_id=ring(1), device_id_type=MESH)

    expected = len(peers) + jnp.where(me > 0, 1, 0) + jnp.where(me < 127, 1, 0)

    def start_rest():
        load("rs2", rs_hbm, rhi.at[pl.ds(0, 16)])
        load("ns", ns_hbm, ns)
        load("nc", nc_hbm, nc)
        load("cs", cs_hbm, cs)
        load("cc", cc_hbm, cc)
        load("ts", ts_hbm, ts)
        load("ms", ms_hbm, msv.at[mine])
        load("cp", cp_hbm, cp)
        for place in range(LINE):
            load(f"tb{place}", tb_hbm.at[top_of(place)], tb.at[place])
        load("ld", ld_hbm, ld)
        load("rb", rb_hbm, rb)
        for t in range(16):
            pltpu.make_async_copy(nb_hbm.at[t], nb.at[t], nb_sem.at[t]).start()

    def top_of(place):
        return pick(place * 8 + z * 2, x * 8 + place * 2) + y // 2

    def skeletons():
        for l in range(16):
            skw[8 + l] = dot_nt(cb[l], rlo[8 + l]).astype(BF16)
        loads["mu"].wait()
        lift = None
        for m in range(2):
            raised = dot(ust[m], skw[8 + 8 * m : 16 + 8 * m].reshape(512, 128)).astype(BF16)
            mown[m] = raised
            lifted = dot(mu[m], raised).astype(BF16).astype(F32)
            lift = lifted if lift is None else lift + lifted
        mown[2] = lift.astype(BF16)

    def send_y():
        copies["y"] = [
            send(mown, g1.at[y], y_send.at[k - 1], y_recv.at[k - 1], y_dev(k)) for k in range(1, LINE)
        ]

    def send_skel():
        copies["skel"] = exchange(skw, skw, 24, skel_send, skel_recv)

    def send_halo():
        copies["halo"] = exchange(rlo, rhi, 16, halo_send, halo_recv)

    def exchange(window, above, at, send_sem, recv_sem):
        down = pltpu.make_async_remote_copy(
            src_ref=window.at[pl.ds(8, 8)], dst_ref=above.at[pl.ds(at, 8)],
            send_sem=send_sem.at[0], recv_sem=recv_sem.at[0], device_id=ring(-1), device_id_type=MESH,
        )
        up = pltpu.make_async_remote_copy(
            src_ref=window.at[pl.ds(16, 8)], dst_ref=window.at[pl.ds(0, 8)],
            send_sem=send_sem.at[1], recv_sem=recv_sem.at[1], device_id=ring(1), device_id_type=MESH,
        )
        pl.when(gy % 8 != 0)(down.start)
        pl.when(gy % 8 != 7)(up.start)
        return down, up

    def send_late(name):
        down, up = copies[name]
        pl.when(jnp.logical_and(gy % 8 == 0, me > 0))(down.start)
        pl.when(jnp.logical_and(gy % 8 == 7, me < 127))(up.start)

    def wait_window(name):
        down, up = copies[name]
        pl.when(me < 127)(down.wait_recv)
        pl.when(me > 0)(up.wait_recv)

    def stack_q():
        loads["mb"].wait()
        loads["md"].wait()
        for m in range(2):
            qown[:, 256 * m : 256 * m + 256] = jnp.concatenate([mb[m, k] for k in range(4)], axis=1)
        qown[:, 512:] = jnp.concatenate([md[0], md[1]], axis=1)

    def send_q():
        slot0, slot1 = x * 2 + c, z * 2 + c
        for k in range(1, LINE):
            for core in range(2):
                device = tuple(jnp.where(along_x(core), a, b) for a, b in zip(x_dev(k, core), z_dev(k, core)))
                slot = jnp.where(along_x(core), slot0, slot1)
                at = 2 * (k - 1) + core
                sem = 2 * (k - 1) + c
                sent.append(send(qown, qin.at[slot], q_send.at[at], q_recv.at[sem], device))
                sent.append(send(ms_hbm, msv.at[slot], i_send.at[at], i_recv.at[sem], device))
        slot = jnp.where(along_x(1 - c), slot0, slot1)
        sent.append(send(qown, qin.at[slot], q_send.at[6], q_recv.at[6], sibling))
        sent.append(send(ms_hbm, msv.at[slot], i_send.at[6], i_recv.at[6], sibling))
        qin[mine] = qown[...]

    def stack_t():
        for place in range(LINE):
            loads[f"tb{place}"].wait()
            tst[place] = jnp.concatenate([tb[place, k] for k in range(4)], axis=1)

    def send_g():
        g1[y] = mown[...]
        for copy in copies["y"]:
            copy.wait_recv()
        for p in range(4):
            for m in range(2):
                g2[w * PER + 2 * p + m] = g1[p, m]
        for h in range(2):
            g2[w * PER + 8 + h] = (g1[2 * h, 2].astype(F32) + g1[2 * h + 1, 2].astype(F32)).astype(BF16)
        half = PER // 2
        up, down = on_gather(lax.rem(w + 1, LINE)), on_gather(lax.rem(w + 3, LINE))
        low, high = g2.at[pl.ds(w * PER, half)], g2.at[pl.ds(w * PER + half, half)]
        copies["g"] = [
            send(part, part, g_send.at[at], g_recv.at[at], device)
            for at, (part, device) in enumerate(((low, up), (high, down), (high, up), (low, down)))
        ]

    def forward_g():
        half = PER // 2
        up, down = on_gather(lax.rem(w + 1, LINE)), on_gather(lax.rem(w + 3, LINE))
        for at, place, start, device in ((0, w + 3, 0, up), (1, w + 1, half, down)):
            copies["g"][at].wait_recv()
            part = g2.at[pl.ds(lax.rem(place, LINE) * PER + start, half)]
            copies["g"].append(send(part, part, g_send.at[4 + at], g_recv.at[4 + at], device))

    def stack_c():
        loads["cp"].wait()
        for t in range(16):
            cst[t] = jnp.concatenate([cp[t, k] for k in range(8)], axis=1)

    def couple():
        wait_window("skel")
        loads["cs"].wait()
        loads["cc"].wait()
        for t in range(16):
            rows = []
            for k in range(8):
                row = skw[jnp.clip(cs[k, t] - base, 0, 31)]
                rows.append(jnp.where(k < cc[t], row, jnp.zeros_like(row)))
            leaf_far[t] = dot(cst[t], jnp.concatenate(rows, axis=0))

    def fold():
        for at in range(7):
            arrived(qown, qin.at[0], q_send.at[at], q_recv.at[at])
            arrived(ms_hbm, msv.at[0], i_send.at[at], i_recv.at[at])
        loads["ms"].wait()
        loads["ts"].wait()
        tables = pltpu.make_async_copy(msv, mss, out_sem.at[0])
        tables.start()
        lane = lax.broadcasted_iota(jnp.int32, (64, 128), 1)
        for s in range(8):
            down = qin[s, :, 512:]
            zero = jnp.zeros_like(down)
            both = jnp.concatenate(
                [jnp.where(lane < 64, down, zero), jnp.where(lane < 64, zero, down)], axis=0
            )
            folded = dot(both, jnp.concatenate([tst[s // 2], tst[s // 2]], axis=0)).astype(BF16)
            for m in range(2):
                qfull[s, m, :, :256] = qin[s, :, 256 * m : 256 * m + 256]
                qfull[s, m, :, 256:] = folded[64 * m : 64 * m + 64]
        tables.wait()
        g2[LINE * PER] = jnp.zeros((64, 128), BF16)
        for i in range(4):
            for s in range(8):
                for m in range(2):
                    mix[s, m, i] = mid_at(mss[s, m, i])
            for place in range(LINE):
                tix[place, i] = top_at(ts[i, top_of(place)])

    def near(window, start, shift):
        def step(i, carry):
            t = start + i
            total = jnp.zeros((128, 256), F32)
            for k in range(8):
                side = window[jnp.clip(ns[k, t] - shift, 0, 23)]
                total += dot_nt(jnp.where(k < nc[t], side, jnp.zeros_like(side)), nb[t, k])
            acc[t] = total
            return carry

        lax.fori_loop(0, 8, step, 0)

    def near_low():
        pl.when(me > 0)(copies["halo"][1].wait_recv)
        near(rlo, 0, me * 16 - 8)

    def near_high():
        pl.when(me < 127)(copies["halo"][0].wait_recv)
        near(rhi, 8, me * 16)

    def near_fast():
        pl.when(first)(near_high)
        pl.when(c == 1)(near_low)

    def near_slow():
        pl.when(first)(near_low)
        pl.when(c == 1)(near_high)

    def wait_near():
        loads["rs2"].wait()
        loads["ns"].wait()
        loads["nc"].wait()
        for t in range(16):
            pltpu.make_async_copy(nb_hbm.at[t], nb.at[t], nb_sem.at[t]).wait()

    def mid_at(m):
        dev = m // 2
        mx, mz, my, mc = dev // 32, (dev // 8) % 4, (dev // 2) % 4, dev % 2
        held = (mc == c) & (pick(mx, mz) == v)
        return jnp.where(held, pick(mz, mx) * PER + my * 2 + m % 2, LINE * PER)

    def top_at(n):
        nx, nz = n // 8, (n // 2) % 4
        return jnp.where(pick(nx, nz) == v, pick(nz, nx) * PER + 8 + n % 2, LINE * PER)

    def serve():
        for copy in copies["g"][2:]:
            copy.wait_recv()
        for k in range(1, LINE + 1):
            place = lax.rem(v + k, LINE)
            tops = [g2[tix[place, i]] for i in range(4)]
            for core in range(2):
                s = 2 * place + core
                for m in range(2):
                    rows = [g2[mix[s, m, i]] for i in range(4)]
                    psend[s, m] = dot(qfull[s, m], jnp.concatenate(rows + tops, axis=0)).astype(BF16)
                if k < LINE:
                    at = 2 * (k - 1) + core
                    sent.append(
                        send(psend.at[s], precv.at[4 * c + v], p_send.at[at], p_recv.at[3 * c + k - 1],
                             on_line(place, core))
                    )
        sent.append(
            send(psend.at[2 * v + 1 - c], precv.at[4 * c + v], p_send.at[6], p_recv.at[6], sibling)
        )
        precv[4 * c + v] = psend[mine]

    def lower():
        loads["ld"].wait()
        loads["rb"].wait()
        for at in range(7):
            arrived(psend.at[0], precv.at[0], p_send.at[at], p_recv.at[at])
        for m in range(2):
            total = precv[0, m].astype(F32)
            for s in range(1, 8):
                total += precv[s, m].astype(F32)
            lowered = dot(ld[8 * m : 8 * m + 8].reshape(512, 64), total.astype(BF16))
            for l in range(8):
                t = 8 * m + l
                local = (leaf_far[t] + lowered[64 * l : 64 * l + 64]).astype(BF16)
                out[t] = (acc[t] + dot_tn(local, rb[t])).astype(BF16)

    def finish():
        for copy in sent + copies["y"] + copies["g"]:
            copy.wait_send()
        for name in ("skel", "halo"):
            down, up = copies[name]
            pl.when(me > 0)(down.wait_send)
            pl.when(me < 127)(up.wait_send)

    copies, sent = {}, []
    mine = 2 * v + c
    base = me * 16 - 8
    loads["lu"].wait()
    for m in range(2):
        ust[m] = jnp.concatenate([lu[8 * m + l] for l in range(8)], axis=1)
    loads["rs"].wait()
    loads["cb"].wait()
    start_rest()
    skeletons()
    pl.semaphore_wait(barrier, expected)
    send_y()
    send_halo()
    send_skel()
    send_late("skel")
    stack_q()
    send_q()
    stack_t()
    send_g()
    stack_c()
    forward_g()
    send_late("halo")
    fold()
    wait_near()
    near_fast()
    serve()
    couple()
    near_slow()
    lower()
    finish()


def local(*args):
    args = list(args)
    for at in (1, 7, 13):
        args[at] = args[at].T
    vmem = pltpu.VMEM
    smem = pltpu.SMEM
    dma = pltpu.SemaphoreType.DMA
    scratch = [
        vmem((24, 128, 256), BF16),
        vmem((24, 128, 256), BF16),
        vmem((16, 8, 256, 256), BF16),
        vmem((16, 64, 256), BF16),
        vmem((16, 64, 256), BF16),
        vmem((16, 64, 64), BF16),
        vmem((16, 8, 64, 64), BF16),
        vmem((2, 64, 64), BF16),
        vmem((2, 4, 64, 64), BF16),
        vmem((4, 4, 64, 64), BF16),
        vmem((2, 64, 64), BF16),
        vmem((16, 64, 64), BF16),
        smem((8, 16), jnp.int32),
        smem((16,), jnp.int32),
        smem((8, 16), jnp.int32),
        smem((16,), jnp.int32),
        smem((4, 32), jnp.int32),
        smem((8, 2, 4), jnp.int32),
        smem((8, 2, 4), jnp.int32),
        smem((4, 4), jnp.int32),
        vmem((8, 2, 4), jnp.int32),
        vmem((32, 64, 128), BF16),
        vmem((2, 64, 512), BF16),
        vmem((16, 64, 512), BF16),
        vmem((4, 64, 256), BF16),
        vmem((64, 640), BF16),
        vmem((8, 64, 640), BF16),
        vmem((8, 2, 64, 512), BF16),
        vmem((3, 64, 128), BF16),
        vmem((4, 3, 64, 128), BF16),
        vmem((4 * PER + 1, 64, 128), BF16),
        vmem((8, 2, 64, 128), BF16),
        vmem((8, 2, 64, 128), BF16),
        vmem((16, 64, 128), F32),
        vmem((16, 128, 256), F32),
        dma((20,)), dma((16,)), dma((1,)),
        dma((2,)), dma((2,)), dma((2,)), dma((2,)),
        dma((7,)), dma((7,)), dma((7,)), dma((7,)),
        dma((3,)), dma((3,)), dma((6,)), dma((6,)),
        dma((7,)), dma((7,)),
    ]
    return pl.pallas_call(
        kernel,
        out_shape=jax.ShapeDtypeStruct((16, 128, 256), BF16),
        in_specs=[pl.BlockSpec(memory_space=pl.ANY)] * len(args),
        out_specs=pl.BlockSpec(memory_space=pltpu.VMEM),
        scratch_shapes=scratch,
        compiler_params=pltpu.CompilerParams(
            collective_id=0, has_side_effects=True, vmem_limit_bytes=56 * 1024 * 1024
        ),
    )(*args)


def solution(mesh):
    both = ("gx", "gy")
    placed = [P(both)] * 17
    placed[13] = placed[14] = P()
    return jax.shard_map(
        local, mesh=mesh, in_specs=tuple(placed), out_specs=P(both), check_vma=False
    )
```
